32 devices in a mesh: dom: 8 (over z, x), cls: 4 (over y, core).
Axes of the slice: x: 2, y: 2, z: 4, core: 2. Of those that a mesh axis runs over, the one named last changes fastest.
Arguments:
- images: bfloat16 [768, 13824], P('dom')
- pick_counts: int32 [8], replicated, may hold values from 0 to 96, as said below
- group_of: int32 [768], replicated, may hold values from 0 to 31
- ctf_table: float32 [32, 32], replicated, may hold values from -1 to 1
- precision: float32 [32], replicated, may hold values from 0.1 to 1
- references: bfloat16 [200, 13824], P('cls')
Outputs:
- new_refs: float32 [200, 13824], P('cls', 'dom')
- confidence: float32 [768], P('dom')
The draws below stay inside these ranges and needn't reach their ends.
Inputs may be any that keep to these rules, and one draw needn't show every extreme that they name: `pick_counts`: the counts sum to 384; each reader and the reader half of the dom axis away hold 96 particles together, and some reader holds exactly 96.
All inputs are finite; a program needn't handle non-finite values.
Results may differ from the reference program's by a relative error of at most 0.0037.
Values may be sent and summed in bfloat16 or wider, within the bound.
A program may use at most 320 MiB of HBM per device.

```python
import math
import jax
import jax.numpy as jnp
from jax import lax

K = 200
ROT = 36
CYCLES = 32
ANG = 216
GROUPS = 32
OWN = 48
READ = 96
STEP = 6
FEAT = 13824
ROWS = 768
N_DOM = 8


def make_classes(key):
    grid_shape = (K, CYCLES, ANG, 2)
    magnitude = math.sqrt(10.6 * math.log(ROT * K) / FEAT)
    class_gain = jax.random.uniform(jax.random.fold_in(key, 51), (K, 1, 1, 1), jnp.float32, 0.9, 1.1)
    entries = jax.random.uniform(jax.random.fold_in(key, 52), grid_shape, jnp.float32, 0.75, 1.25)
    cycle_gain = jax.random.uniform(jax.random.fold_in(key, 53), (K, CYCLES, 1, 1), jnp.float32, 0.85, 1.15)
    sign_field = (2 * jax.random.randint(jax.random.fold_in(key, 54), grid_shape, 0, 2) - 1).astype(jnp.float32)
    return magnitude * class_gain * cycle_gain * entries * sign_field


def make_ctf(key):
    return jax.random.uniform(jax.random.fold_in(key, 61), (GROUPS, CYCLES), jnp.float32, -1.0, 1.0)


def make_groups(key):
    return jax.random.randint(jax.random.fold_in(key, 62), (ROWS,), 0, GROUPS).astype(jnp.int32)


def rotate_rows(classes, chosen, turn_count):
    angle_index = (jnp.arange(ANG, dtype=jnp.int32)[None, :] - turn_count[:, None] * STEP) % ANG
    picked = classes[chosen[:, None], :, angle_index]
    return jnp.transpose(picked, (0, 2, 1, 3))


def make_images(key):
    classes = make_classes(key)
    ctf_values = make_ctf(key)
    groups = make_groups(key)
    grid_shape = (ROWS, CYCLES, ANG, 2)
    chosen = jax.random.randint(jax.random.fold_in(key, 71), (ROWS,), 0, K).astype(jnp.int32)
    turn_count = jax.random.randint(jax.random.fold_in(key, 72), (ROWS,), 0, ROT).astype(jnp.int32)
    ctf_rows = ctf_values[groups][:, :, None, None]
    signal = rotate_rows(classes, chosen, turn_count)
    noise_field = jnp.clip(jax.random.normal(jax.random.fold_in(key, 73), grid_shape, jnp.float32), -5.0, 5.0)
    drawn_rows = ctf_rows * signal + noise_field
    strong = jax.random.randint(jax.random.fold_in(key, 75), (ROWS,), 0, 32) == 0
    second_class = ((chosen + 1 + jax.random.randint(jax.random.fold_in(key, 76), (ROWS,), 0, K - 1)) % K).astype(jnp.int32)
    second_turn = jax.random.randint(jax.random.fold_in(key, 77), (ROWS,), 0, ROT).astype(jnp.int32)
    levels = jnp.array([16.0, 32.0, 48.0, 64.0], jnp.float32)
    strength = levels[jax.random.randint(jax.random.fold_in(key, 78), (ROWS,), 0, 4)]
    mixed_rows = strength[:, None, None, None] * ctf_rows * 0.5 * (signal + rotate_rows(classes, second_class, second_turn)) + 0.2 * noise_field
    return jnp.where(strong[:, None, None, None], mixed_rows, drawn_rows).reshape(ROWS, FEAT)


def draw_images(key, part):
    return make_images(key).astype(jnp.bfloat16)


def draw_references(key, part):
    return make_classes(key).reshape(K, FEAT).astype(jnp.bfloat16)


def draw_ctf_table(key, part):
    return make_ctf(key)


def draw_group_of(key, part):
    return make_groups(key)


def draw_pick_counts(key, part):
    half_axis = N_DOM // 2
    excess = jax.random.randint(jax.random.fold_in(key, 12), (half_axis,), 0, OWN + 1)
    full_pair = jax.random.randint(jax.random.fold_in(key, 13), (), 0, half_axis)
    excess = jnp.where(jnp.arange(half_axis, dtype=jnp.int32) == full_pair, OWN, excess)
    direction = 2 * jax.random.randint(jax.random.fold_in(key, 14), (half_axis,), 0, 2) - 1
    first_half = OWN + direction * excess
    second_half = OWN - direction * excess
    return jnp.concatenate([first_half, second_half]).astype(jnp.int32)


def setup_inputs(seed: int = 0) -> dict:
    key_of = jax.random.split(jax.random.key(seed), 7)
    images = draw_images(jax.random.fold_in(key_of[6], 71), 0)
    pick_counts = draw_pick_counts(jax.random.fold_in(key_of[6], 71), 0)
    group_of = draw_group_of(jax.random.fold_in(key_of[6], 71), 0)
    ctf_table = draw_ctf_table(jax.random.fold_in(key_of[6], 71), 0)
    precision = jnp.clip(jnp.exp(jax.random.uniform(key_of[4], (CYCLES,), jnp.float32, math.log(0.1), math.log(1.0))), 0.1, 1.0)
    references = draw_references(jax.random.fold_in(key_of[6], 71), 0)
    return {"images": images, "pick_counts": pick_counts, "group_of": group_of, "ctf_table": ctf_table, "precision": precision, "references": references}


ridge_term = 0.02


def reference(images, pick_counts, group_of, ctf_table, precision, references):
    total_rows = OWN * N_DOM
    ends_at = jnp.cumsum(pick_counts).astype(jnp.int32)
    starts = (ends_at - pick_counts).astype(jnp.int32)
    order_rank = jnp.arange(total_rows, dtype=jnp.int32)
    source = jnp.sum((ends_at[None, :] <= order_rank[:, None]).astype(jnp.int32), axis=1).astype(jnp.int32)
    position = order_rank - starts[source]
    flat_row = (source * READ + position).astype(jnp.int32)
    pixels = images[flat_row]
    groups = group_of[flat_row]
    ctf_rows = ctf_table[groups]
    cycle_scale = precision[None, :] * ctf_rows
    ctf_power = precision[None, :] * jnp.square(ctf_rows)
    shaped = pixels.reshape(total_rows, CYCLES, 2 * ANG).astype(jnp.float32)
    weighted = (cycle_scale[:, :, None] * shaped).astype(jnp.bfloat16).reshape(total_rows, FEAT)
    shaped_refs = references.reshape(K, CYCLES, 2 * ANG)
    energy = jnp.sum(jnp.square(shaped_refs.astype(jnp.float32)), axis=2)
    ref_power = jnp.dot(ctf_power, energy.T, precision=lax.Precision.HIGHEST)
    correlation = jnp.stack([jnp.dot(weighted, jnp.roll(shaped_refs, 2 * turn * STEP, axis=2).reshape(K, FEAT).T, preferred_element_type=jnp.float32) for turn in range(ROT)], axis=1)
    logits = correlation - 0.5 * ref_power[:, None, :]
    peak_logit = jnp.max(logits, axis=(1, 2))
    shifted = jnp.exp(logits - peak_logit[:, None, None])
    mass_total = jnp.sum(shifted, axis=(1, 2))
    posterior = shifted / mass_total[:, None, None]
    post_bf = posterior.astype(jnp.bfloat16)
    numerator = jnp.zeros((K, CYCLES, 2 * ANG), jnp.float32)
    for turn in range(ROT):
        partial_sum = jnp.dot(post_bf[:, turn, :].T, weighted, preferred_element_type=jnp.float32)
        numerator = numerator + jnp.roll(partial_sum.reshape(K, CYCLES, 2 * ANG), -2 * turn * STEP, axis=2)
    onehot = (groups[:, None] == jnp.arange(GROUPS, dtype=jnp.int32)[None, :]).astype(jnp.float32)
    weights = jnp.dot(jnp.sum(posterior, axis=1).T, onehot, precision=lax.Precision.HIGHEST)
    denominator = precision[None, :] * jnp.dot(weights, jnp.square(ctf_table), precision=lax.Precision.HIGHEST)
    new_refs = (numerator / (denominator[:, :, None] + ridge_term)).reshape(K, FEAT)
    confidence = jnp.zeros((READ * N_DOM,), jnp.float32).at[flat_row].set(1.0 / mass_total)
    return new_refs, confidence
```

```python
import functools

import jax
import jax.numpy as jnp
from jax import lax
from jax.experimental import pallas as pl
from jax.experimental.pallas import tpu as pltpu
from jax.sharding import PartitionSpec as P

CYCLES = 32
WIDE = 432
TURN = 12
FINE = 4
BLOCK = TURN * FINE
COARSE = WIDE // BLOCK
BUNCH = 8
DEPTH = CYCLES * BLOCK
SLOT = 64
ridge_term = 0.02
HIGH = lax.Precision.HIGHEST
f32 = jnp.float32
bf16 = jnp.bfloat16


def score_kernel(img, groups, ctf, precision, refs, twice, spread, stats, power, turned):
    rows = img.shape[0]
    classes = refs.shape[0]
    kinds = ctf.shape[0]
    group = groups[...]
    onehot = (group == lax.broadcasted_iota(jnp.int32, (rows, kinds), 1)).astype(f32)
    ctf_rows = jnp.dot(onehot, ctf[...], precision=HIGH, preferred_element_type=f32)
    prec = precision[...]
    scale = prec * ctf_rows
    ctf_power = prec * jnp.square(ctf_rows)
    power[...] = ctf_power

    fill = jnp.zeros((SLOT - classes, BUNCH * WIDE), bf16)
    energies = []
    for bunch in range(CYCLES // BUNCH):
        lanes = slice(bunch * BUNCH * WIDE, (bunch + 1) * BUNCH * WIDE)
        out = slice(bunch * BUNCH * BLOCK, (bunch + 1) * BUNCH * BLOCK)
        factor = jnp.concatenate(
            [
                jnp.broadcast_to(scale[:, c : c + 1], (rows, BLOCK))
                for c in range(bunch * BUNCH, (bunch + 1) * BUNCH)
            ],
            axis=1,
        )
        pixels = img[:, lanes]
        for s in range(COARSE):
            piece = jnp.concatenate(
                [
                    pixels[:, c * WIDE + s * BLOCK : c * WIDE + (s + 1) * BLOCK]
                    for c in range(BUNCH)
                ],
                axis=1,
            )
            value = (piece.astype(f32) * factor).astype(bf16)
            twice[s * rows : (s + 1) * rows, out] = value
            if s < COARSE - 1:
                twice[(s + COARSE) * rows : (s + COARSE + 1) * rows, out] = value
        block = jnp.concatenate([refs[:, lanes], fill], axis=0)
        for c in range(BUNCH):
            one = block[:, c * WIDE : (c + 1) * WIDE].astype(f32)
            energies.append(jnp.sum(one * one, axis=1, keepdims=True))
        for s in range(COARSE):
            for turn in range(FINE):
                parts = []
                for c in range(BUNCH):
                    first = s * BLOCK - turn * TURN
                    base = c * WIDE
                    if first < 0:
                        parts.append(block[:, base + WIDE + first : base + WIDE])
                        parts.append(block[:, base : base + first + BLOCK])
                    else:
                        parts.append(block[:, base + first : base + first + BLOCK])
                turned[s, turn * SLOT : (turn + 1) * SLOT, out] = jnp.concatenate(parts, axis=1)

    energy = jnp.concatenate(energies, axis=1)
    ref_power = lax.dot_general(
        ctf_power, energy, (((1,), (1,)), ((), ())), precision=HIGH, preferred_element_type=f32
    )
    half = 0.5 * jnp.concatenate([ref_power] * FINE, axis=1)

    spread[...] = jnp.zeros_like(spread)

    @pl.loop(0, COARSE)
    def _(s):
        start = pl.multiple_of(s * rows, 16)
        spread[...] += lax.dot_general(
            twice[pl.ds(start, COARSE * rows), :],
            turned[s],
            (((1,), (1,)), ((), ())),
            preferred_element_type=f32,
        )

    real = lax.broadcasted_iota(jnp.int32, (rows, FINE * SLOT), 1) % SLOT < classes
    highest = jnp.full((rows, FINE * SLOT), -jnp.inf, f32)
    for g in range(COARSE):
        part = slice(g * rows, (g + 1) * rows)
        logits = jnp.where(real, spread[part, :] - half, -jnp.inf)
        spread[part, :] = logits
        highest = jnp.maximum(highest, logits)
    peak = jnp.max(highest, axis=1, keepdims=True)
    total = jnp.zeros((rows, FINE * SLOT), f32)
    for g in range(COARSE):
        part = slice(g * rows, (g + 1) * rows)
        raised = jnp.exp(spread[part, :] - peak)
        spread[part, :] = raised
        total = total + raised
    mass = jnp.sum(total, axis=1, keepdims=True)
    lane = lax.broadcasted_iota(jnp.int32, (rows, 128), 1)
    stats[...] = jnp.where(lane == 0, peak, mass)


def sum_kernel(twice, spread, factor, power, out, chosen, sums):
    rows = factor.shape[0]
    parts, classes, width = out.shape
    share = CYCLES // parts
    times = factor[...]
    total = jnp.zeros((rows, FINE * SLOT), f32)
    for g in range(COARSE):
        part = slice(g * rows, (g + 1) * rows)
        posterior = spread[part, :] * times
        spread[part, :] = posterior
        total = total + posterior
    chosen[...] = spread[...].T.astype(bf16)
    weight = total[:, :SLOT]
    for turn in range(1, FINE):
        weight = weight + total[:, turn * SLOT : (turn + 1) * SLOT]
    denominator = jnp.dot(weight.T, power[...], precision=HIGH, preferred_element_type=f32)

    @pl.loop(0, COARSE)
    def _(s):
        start = pl.multiple_of(s * rows, 16)
        sums[s] = jnp.dot(
            chosen[...], twice[pl.ds(start, COARSE * rows), :], preferred_element_type=f32
        )

    place = lax.broadcasted_iota(jnp.int32, (SLOT, DEPTH), 1) % BLOCK

    def fold(s):
        kept = sums[s, :SLOT, :]
        over = jnp.zeros((SLOT, DEPTH), f32)
        for turn in range(1, FINE):
            moved = pltpu.roll(
                sums[s, turn * SLOT : (turn + 1) * SLOT, :], DEPTH - turn * TURN, 1
            )
            inside = place < BLOCK - turn * TURN
            kept = kept + jnp.where(inside, moved, 0.0)
            over = over + jnp.where(inside, 0.0, moved)
        return kept, pltpu.roll(over, BLOCK, 1)

    overs = []
    for s in range(COARSE):
        kept, over = fold(s)
        sums[s, :SLOT, :] = kept
        sums[s, SLOT : 2 * SLOT, :] = over
    upper = denominator.astype(bf16)
    lower = (denominator - upper.astype(f32)).astype(bf16)
    tail = jnp.zeros((SLOT, width - share * (WIDE + 2)), bf16)
    blocks = [
        (sums[s, :SLOT, :] + sums[(s + 1) % COARSE, SLOT : 2 * SLOT, :]).astype(bf16)
        for s in range(COARSE)
    ]
    for d in range(parts):
        pieces = [b[:, d * share * BLOCK : (d + 1) * share * BLOCK] for b in blocks]
        cycles = slice(d * share, (d + 1) * share)
        whole = jnp.concatenate(pieces + [upper[:, cycles], lower[:, cycles], tail], axis=1)
        out[d] = whole[:classes]


def finish_kernel(parts, out):
    count = parts.shape[0]
    share = out.shape[1] // WIDE
    total = parts[0].astype(f32)
    for d in range(1, count):
        total = total + parts[d].astype(f32)
    end = share * WIDE
    denominator = total[:, end : end + share] + total[:, end + share : end + 2 * share]
    cycles = []
    for c in range(share):
        numerator = jnp.concatenate(
            [
                total[:, (s * share + c) * BLOCK : (s * share + c + 1) * BLOCK]
                for s in range(COARSE)
            ],
            axis=1,
        )
        cycles.append(numerator / (denominator[:, c : c + 1] + ridge_term))
    out[...] = jnp.concatenate(cycles, axis=1)


def in_vmem(count):
    return [pl.BlockSpec(memory_space=pltpu.VMEM)] * count


def body(images, pick_counts, group_of, ctf_table, precision, references):
    dom_count = lax.axis_size("dom")
    me = lax.axis_index("dom")
    rows = images.shape[0]
    classes = references.shape[0]
    share = CYCLES // dom_count
    width = -(-share * (WIDE + 2) // 128) * 128
    slots = jnp.arange(rows, dtype=jnp.int32)
    alive = slots < lax.dynamic_index_in_dim(pick_counts, me, 0, False)
    groups = jnp.where(alive, lax.dynamic_slice_in_dim(group_of, me * rows, rows), -1)
    params = pltpu.CompilerParams(vmem_limit_bytes=56 * 2**20)
    twice, spread, stats, power = pl.pallas_call(
        score_kernel,
        out_shape=[
            jax.ShapeDtypeStruct(((2 * COARSE - 1) * rows, DEPTH), bf16),
            jax.ShapeDtypeStruct((COARSE * rows, FINE * SLOT), f32),
            jax.ShapeDtypeStruct((rows, 128), f32),
            jax.ShapeDtypeStruct((rows, CYCLES), f32),
        ],
        in_specs=in_vmem(5),
        out_specs=in_vmem(4),
        scratch_shapes=[pltpu.VMEM((COARSE, FINE * SLOT, DEPTH), bf16)],
        compiler_params=params,
        name="score",
    )(images, groups[:, None], ctf_table, precision[None, :], references)
    peak, mass = stats[:, 0], stats[:, 1]
    all_stats = lax.all_gather(stats[:, :2].T, "cls")
    top = jnp.max(all_stats[:, 0], axis=0)
    mass_total = jnp.sum(all_stats[:, 1] * jnp.exp(all_stats[:, 0] - top[None, :]), axis=0)
    confidence = jnp.where(alive, 1.0 / mass_total, 0.0)
    factor = jnp.where(alive, jnp.exp(peak - top) / mass_total, 0.0)
    partial = pl.pallas_call(
        sum_kernel,
        out_shape=jax.ShapeDtypeStruct((dom_count, classes, width), bf16),
        in_specs=in_vmem(4),
        out_specs=pl.BlockSpec(memory_space=pltpu.VMEM),
        scratch_shapes=[
            pltpu.VMEM((FINE * SLOT, COARSE * rows), bf16),
            pltpu.VMEM((COARSE, FINE * SLOT, DEPTH), f32),
        ],
        compiler_params=params,
        name="sums",
    )(twice, spread, factor[:, None], power)
    parts = lax.all_to_all(partial, "dom", split_axis=0, concat_axis=0, tiled=True)
    new_refs = pl.pallas_call(
        finish_kernel,
        out_shape=jax.ShapeDtypeStruct((classes, share * WIDE), f32),
        in_specs=in_vmem(1),
        out_specs=pl.BlockSpec(memory_space=pltpu.VMEM),
        compiler_params=params,
        name="finish",
    )(parts)
    return (new_refs, confidence)


def solution(mesh):
    return jax.shard_map(
        body,
        mesh=mesh,
        in_specs=(P("dom", None), P(), P(), P(), P(), P("cls", None)),
        out_specs=(P("cls", "dom"), P("dom")),
        check_vma=False,
    )
```

```python
import functools

import jax
import jax.numpy as jnp
from jax import lax
from jax.experimental import pallas as pl
from jax.experimental.pallas import tpu as pltpu
from jax.sharding import PartitionSpec as P

CYCLES = 32
WIDE = 432
TURN = 12
FINE = 4
BLOCK = TURN * FINE
COARSE = WIDE // BLOCK
BUNCH = 8
DEPTH = CYCLES * BLOCK
SLOT = 64
ridge_term = 0.02
HIGH = lax.Precision.HIGHEST
f32 = jnp.float32
bf16 = jnp.bfloat16

MESH = pl.DeviceIdType.MESH


def em_kernel(
    parts,
    quads,
    img,
    counts,
    group_rows,
    ctf,
    precision,
    refs,
    out,
    conf,
    twice,
    turned,
    spread,
    chosen,
    fresh,
    kept,
    over,
    first_over,
    mine,
    give,
    take,
    den_mine,
    den_take,
    pass_on,
    land,
    stat_send,
    stat_land,
    stat_ssem,
    stat_rsem,
    give_ssem,
    give_rsem,
    den_ssem,
    den_rsem,
    pass_ssem,
    pass_rsem,
):
    rows = img.shape[0]
    classes = refs.shape[0]
    kinds = ctf.shape[0]
    share = CYCLES // parts
    lines = parts // 2
    half_depth = DEPTH // 2
    me = lax.axis_index("dom")
    my_class = lax.axis_index("cls")
    low, high = lax.rem(me, 2), lax.div(me, 2)
    mate = me + 1 - 2 * low

    barrier = pltpu.get_barrier_semaphore()
    for step in range(1, quads):
        other = lax.rem(my_class + step, quads)
        pl.semaphore_signal(barrier, inc=1, device_id=(me, other), device_id_type=MESH)
    pl.semaphore_signal(barrier, inc=1, device_id=(mate, my_class), device_id_type=MESH)
    for step in range(1, lines):
        other = 2 * lax.rem(high + step, lines) + low
        pl.semaphore_signal(barrier, inc=1, device_id=(other, my_class), device_id_type=MESH)

    order = [
        (h * 2 + l) * share + c for l in range(2) for h in range(lines) for c in range(share)
    ]

    count_lane = lax.broadcasted_iota(jnp.int32, (1, parts), 1)
    count = jnp.sum(jnp.where(count_lane == me, counts[...], 0), axis=1, keepdims=True)
    alive = lax.broadcasted_iota(jnp.int32, (1, rows), 1) < count
    group_row = jnp.where(alive, group_rows[pl.ds(me, 1), :], -1).astype(f32)
    group = jnp.broadcast_to(group_row, (8, rows)).T[:, :1]
    kind = lax.broadcasted_iota(jnp.int32, (rows, kinds), 1).astype(f32)
    onehot = (group == kind).astype(f32)
    ctf_rows = jnp.dot(onehot, ctf[...], precision=HIGH, preferred_element_type=f32)
    prec = precision[...]
    scale = prec * ctf_rows
    ctf_power = prec * jnp.square(ctf_rows)

    fill = jnp.zeros((SLOT - classes, WIDE), bf16)
    energies = [None] * CYCLES
    for bunch in range(CYCLES // BUNCH):
        lane_out = slice(bunch * BUNCH * BLOCK, (bunch + 1) * BUNCH * BLOCK)
        names = order[bunch * BUNCH : (bunch + 1) * BUNCH]
        factor = jnp.concatenate(
            [jnp.broadcast_to(scale[:, c : c + 1], (rows, BLOCK)) for c in names], axis=1
        )
        pixels = [img[:, c * WIDE : (c + 1) * WIDE] for c in names]
        for s in range(COARSE):
            piece = jnp.concatenate([p[:, s * BLOCK : (s + 1) * BLOCK] for p in pixels], axis=1)
            value = (piece.astype(f32) * factor).astype(bf16)
            twice[s * rows : (s + 1) * rows, lane_out] = value
            if s < COARSE - 1:
                twice[(s + COARSE) * rows : (s + COARSE + 1) * rows, lane_out] = value
        block = [
            jnp.concatenate([refs[:, c * WIDE : (c + 1) * WIDE], fill], axis=0) for c in names
        ]
        for c, b in zip(names, block):
            wide = b.astype(f32)
            energies[c] = jnp.sum(wide * wide, axis=1, keepdims=True)
        for s in range(COARSE):
            for turn in range(FINE):
                pieces = []
                first = s * BLOCK - turn * TURN
                for b in block:
                    if first < 0:
                        pieces.append(b[:, WIDE + first :])
                        pieces.append(b[:, : first + BLOCK])
                    else:
                        pieces.append(b[:, first : first + BLOCK])
                turned[s, turn * SLOT : (turn + 1) * SLOT, lane_out] = jnp.concatenate(
                    pieces, axis=1
                )

    energy = jnp.concatenate(energies, axis=1)
    ref_power = lax.dot_general(
        ctf_power, energy, (((1,), (1,)), ((), ())), precision=HIGH, preferred_element_type=f32
    )
    half = 0.5 * jnp.concatenate([ref_power] * FINE, axis=1)

    spread[...] = jnp.zeros_like(spread)

    @pl.loop(0, COARSE)
    def _(s):
        start = pl.multiple_of(s * rows, 16)
        spread[...] += lax.dot_general(
            twice[pl.ds(start, COARSE * rows), :],
            turned[s],
            (((1,), (1,)), ((), ())),
            preferred_element_type=f32,
        )

    real = lax.broadcasted_iota(jnp.int32, (rows, FINE * SLOT), 1) % SLOT < classes
    highest = jnp.full((rows, FINE * SLOT), -jnp.inf, f32)
    for g in range(COARSE):
        part = slice(g * rows, (g + 1) * rows)
        logits = jnp.where(real, spread[part, :] - half, -jnp.inf)
        spread[part, :] = logits
        highest = jnp.maximum(highest, logits)
    peak = jnp.max(highest, axis=1, keepdims=True)
    total = jnp.zeros((rows, FINE * SLOT), f32)
    for g in range(COARSE):
        part = slice(g * rows, (g + 1) * rows)
        raised = jnp.exp(spread[part, :] - peak)
        spread[part, :] = raised
        total = total + raised
    mass = jnp.sum(total, axis=1, keepdims=True)
    lane = lax.broadcasted_iota(jnp.int32, (rows, 128), 1)
    stat_send[...] = jnp.where(lane == 0, peak, mass).T[:8, :]

    pl.semaphore_wait(barrier, quads - 1 + lines)
    stat_copies = []
    for step in range(1, quads):
        other = lax.rem(my_class + step, quads)
        copy = pltpu.make_async_remote_copy(
            src_ref=stat_send,
            dst_ref=stat_land.at[step - 1],
            send_sem=stat_ssem.at[step - 1],
            recv_sem=stat_rsem.at[step - 1],
            device_id=(me, other),
            device_id_type=MESH,
        )
        copy.start()
        stat_copies.append(copy)
    for copy in stat_copies:
        copy.wait()
    own_stat = stat_send[...]
    everyone = [own_stat] + [stat_land[i] for i in range(quads - 1)]
    top = everyone[0][:1]
    for stat in everyone[1:]:
        top = jnp.maximum(top, stat[:1])
    mass_total = jnp.zeros_like(top)
    for stat in everyone:
        mass_total = mass_total + stat[1:2] * jnp.exp(stat[:1] - top)
    conf[...] = jnp.where(alive, 1.0 / mass_total, 0.0)
    lower_by = jnp.where(alive, jnp.exp(own_stat[:1] - top) / mass_total, 0.0)
    times = jnp.broadcast_to(lower_by, (8, rows)).T[:, :1]

    total = jnp.zeros((rows, FINE * SLOT), f32)
    for g in range(COARSE):
        part = slice(g * rows, (g + 1) * rows)
        posterior = spread[part, :] * times
        spread[part, :] = posterior
        total = total + posterior
    chosen[...] = spread[...].T.astype(bf16)
    weight = total[:, :SLOT]
    for turn in range(1, FINE):
        weight = weight + total[:, turn * SLOT : (turn + 1) * SLOT]
    den = jnp.dot(weight.T, ctf_power, precision=HIGH, preferred_element_type=f32)
    den_mine[...] = jnp.concatenate([den, jnp.zeros((SLOT, 128 - CYCLES), f32)], axis=1)
    den_copy = pltpu.make_async_remote_copy(
        src_ref=den_mine,
        dst_ref=den_take,
        send_sem=den_ssem.at[0],
        recv_sem=den_rsem.at[0],
        device_id=(mate, my_class),
        device_id_type=MESH,
    )
    den_copy.start()

    place = lax.broadcasted_iota(jnp.int32, (SLOT, DEPTH), 1) % BLOCK

    def give_copy(s):
        return pltpu.make_async_remote_copy(
            src_ref=give.at[s],
            dst_ref=take.at[s],
            send_sem=give_ssem.at[s],
            recv_sem=give_rsem.at[s],
            device_id=(mate, my_class),
            device_id_type=MESH,
        )

    def emit(s, value):
        left, right = value[:classes, :half_depth], value[:classes, half_depth:]
        mine[s] = jnp.where(low == 0, left, right)
        give[s] = jnp.where(low == 0, right, left).astype(bf16)
        give_copy(s).start()

    def pass_copy(j, step):
        other = 2 * lax.rem(high + step, lines) + low
        return pltpu.make_async_remote_copy(
            src_ref=pass_on.at[j, step],
            dst_ref=land.at[j, step - 1],
            send_sem=pass_ssem.at[j, step - 1],
            recv_sem=pass_rsem.at[j, step - 1],
            device_id=(other, my_class),
            device_id_type=MESH,
        )

    wide_pair = pass_on.shape[-1]
    groups = [[s for s in (2 * j, 2 * j + 1) if s < COARSE] for j in range((COARSE + 1) // 2)]

    def forward(j):
        sums = []
        for s in groups[j]:
            give_copy(s).wait_recv()
            sums.append(mine[s] + take[s].astype(f32))
        last = j == len(groups) - 1
        if last:
            den_copy.wait_recv()
            den_all = den_mine[...] + den_take[...]
        for h in range(lines):
            pieces = [v[:, h * share * BLOCK : (h + 1) * share * BLOCK].astype(bf16) for v in sums]
            if last:
                near = den_all[:classes, 2 * h * share : (2 * h + 1) * share]
                far = den_all[:classes, (2 * h + 1) * share : (2 * h + 2) * share]
                some = jnp.where(low == 0, near, far)
                upper = some.astype(bf16)
                pieces += [upper, (some - upper.astype(f32)).astype(bf16)]
            used = sum(p.shape[1] for p in pieces)
            if used < wide_pair:
                pieces.append(jnp.zeros((classes, wide_pair - used), bf16))
            pass_on[j, lax.rem(h - high + lines, lines)] = jnp.concatenate(pieces, axis=1)
        for step in range(1, lines):
            pass_copy(j, step).start()

    for s in range(COARSE):

        @pl.loop(0, DEPTH // 384)
        def _(n):
            columns = pl.ds(pl.multiple_of(n * 384, 128), 384)
            fresh[:, columns] = jnp.dot(
                chosen[...],
                twice[s * rows : (s + COARSE) * rows, columns],
                preferred_element_type=f32,
            )

        stay = fresh[:SLOT, :]
        beyond = jnp.zeros((SLOT, DEPTH), f32)
        for turn in range(1, FINE):
            moved = pltpu.roll(fresh[turn * SLOT : (turn + 1) * SLOT, :], DEPTH - turn * TURN, 1)
            inside = place < BLOCK - turn * TURN
            stay = stay + jnp.where(inside, moved, 0.0)
            beyond = beyond + jnp.where(inside, 0.0, moved)
        beyond = pltpu.roll(beyond, BLOCK, 1)
        if s == 0:
            first_over[...] = beyond
        else:
            emit(s - 1, kept[...] + beyond)
        kept[...] = stay
        if s == COARSE - 1:
            emit(s, kept[...] + first_over[...])
        if s >= 4 and s % 2 == 0:
            forward(s // 2 - 2)
    for j in range(len(groups) - 2, len(groups)):
        forward(j)

    totals = []
    for j in range(len(groups)):
        value = pass_on[j, 0].astype(f32)
        for step in range(1, lines):
            pass_copy(j, step).wait_recv()
            value = value + land[j, step - 1].astype(f32)
        totals.append(value)
    end = share * BLOCK
    tail = totals[-1]
    den_sum = tail[:, end : end + share] + tail[:, end + share : end + 2 * share]
    cycles = []
    for c in range(share):
        numerator = jnp.concatenate(
            [
                totals[s // 2][
                    :, ((s % 2) * share + c) * BLOCK : ((s % 2) * share + c + 1) * BLOCK
                ]
                for s in range(COARSE)
            ],
            axis=1,
        )
        cycles.append(numerator / (den_sum[:, c : c + 1] + ridge_term))
    out[...] = jnp.concatenate(cycles, axis=1)

    den_copy.wait_send()
    for s in range(COARSE):
        give_copy(s).wait_send()
    for j in range(len(groups)):
        for step in range(1, lines):
            pass_copy(j, step).wait_send()


def body(images, pick_counts, group_of, ctf_table, precision, references):
    parts = lax.axis_size("dom")
    quads = lax.axis_size("cls")
    rows = images.shape[0]
    classes = references.shape[0]
    share = CYCLES // parts
    lines = parts // 2
    pairs = (COARSE + 1) // 2
    wide_pair = -(-max(2 * share * BLOCK, share * (BLOCK + 2)) // 128) * 128
    dma = pltpu.SemaphoreType.DMA
    new_refs, confidence = pl.pallas_call(
        functools.partial(em_kernel, parts, quads),
        out_shape=[
            jax.ShapeDtypeStruct((classes, share * WIDE), f32),
            jax.ShapeDtypeStruct((1, rows), f32),
        ],
        in_specs=[pl.BlockSpec(memory_space=pltpu.VMEM)] * 6,
        out_specs=[pl.BlockSpec(memory_space=pltpu.VMEM)] * 2,
        scratch_shapes=[
            pltpu.VMEM(((2 * COARSE - 1) * rows, DEPTH), bf16),
            pltpu.VMEM((COARSE, FINE * SLOT, DEPTH), bf16),
            pltpu.VMEM((COARSE * rows, FINE * SLOT), f32),
            pltpu.VMEM((FINE * SLOT, COARSE * rows), bf16),
            pltpu.VMEM((FINE * SLOT, DEPTH), f32),
            pltpu.VMEM((SLOT, DEPTH), f32),
            pltpu.VMEM((SLOT, DEPTH), f32),
            pltpu.VMEM((SLOT, DEPTH), f32),
            pltpu.VMEM((COARSE, classes, DEPTH // 2), f32),
            pltpu.VMEM((COARSE, classes, DEPTH // 2), bf16),
            pltpu.VMEM((COARSE, classes, DEPTH // 2), bf16),
            pltpu.VMEM((SLOT, 128), f32),
            pltpu.VMEM((SLOT, 128), f32),
            pltpu.VMEM((pairs, lines, classes, wide_pair), bf16),
            pltpu.VMEM((pairs, lines - 1, classes, wide_pair), bf16),
            pltpu.VMEM((8, rows), f32),
            pltpu.VMEM((quads - 1, 8, rows), f32),
            dma((quads - 1,)),
            dma((quads - 1,)),
            dma((COARSE,)),
            dma((COARSE,)),
            dma((1,)),
            dma((1,)),
            dma((pairs, lines - 1)),
            dma((pairs, lines - 1)),
        ],
        compiler_params=pltpu.CompilerParams(
            vmem_limit_bytes=56 * 2**20, collective_id=0, has_side_effects=True
        ),
        name="em",
    )(
        images,
        pick_counts[None, :],
        group_of.reshape(parts, rows),
        ctf_table,
        precision[None, :],
        references,
    )
    return (new_refs, confidence.reshape(rows))


def solution(mesh):
    return jax.shard_map(
        body,
        mesh=mesh,
        in_specs=(P("dom", None), P(), P(), P(), P(), P("cls", None)),
        out_specs=(P("cls", "dom"), P("dom")),
        check_vma=False,
    )
```

```python
import functools

import jax
import jax.numpy as jnp
from jax import lax
from jax.experimental import pallas as pl
from jax.experimental.pallas import tpu as pltpu
from jax.sharding import PartitionSpec as P

CYCLES = 32
WIDE = 432
TURN = 12
FINE = 4
BLOCK = TURN * FINE
COARSE = WIDE // BLOCK
BUNCH = 8
DEPTH = CYCLES * BLOCK
SLOT = 64
ridge_term = 0.02
HIGH = lax.Precision.HIGHEST
f32 = jnp.float32
bf16 = jnp.bfloat16

MESH = pl.DeviceIdType.MESH


def em_kernel(
    parts,
    quads,
    img,
    counts,
    group_rows,
    ctf,
    precision,
    refs,
    out,
    conf,
    twice,
    turned,
    spread,
    chosen,
    fresh,
    kept,
    over,
    first_over,
    mine,
    give,
    take,
    den_mine,
    den_take,
    pass_on,
    land,
    stat_send,
    stat_land,
    stat_ssem,
    stat_rsem,
    give_ssem,
    give_rsem,
    den_ssem,
    den_rsem,
    pass_ssem,
    pass_rsem,
):
    rows = img.shape[0]
    classes = refs.shape[0]
    kinds = ctf.shape[0]
    share = CYCLES // parts
    lines = parts // 2
    half_depth = DEPTH // 2
    me = lax.axis_index("dom")
    my_class = lax.axis_index("cls")
    low, high = lax.rem(me, 2), lax.div(me, 2)
    mate = me + 1 - 2 * low

    barrier = pltpu.get_barrier_semaphore()
    for step in range(1, quads):
        other = lax.rem(my_class + step, quads)
        pl.semaphore_signal(barrier, inc=1, device_id=(me, other), device_id_type=MESH)
    pl.semaphore_signal(barrier, inc=1, device_id=(mate, my_class), device_id_type=MESH)
    for step in range(1, lines):
        other = 2 * lax.rem(high + step, lines) + low
        pl.semaphore_signal(barrier, inc=1, device_id=(other, my_class), device_id_type=MESH)

    order = [
        (h * 2 + l) * share + c for l in range(2) for h in range(lines) for c in range(share)
    ]

    count_lane = lax.broadcasted_iota(jnp.int32, (1, parts), 1)
    count = jnp.sum(jnp.where(count_lane == me, counts[...], 0), axis=1, keepdims=True)
    alive = lax.broadcasted_iota(jnp.int32, (1, rows), 1) < count
    mine_row = group_rows[:, :rows]
    for d in range(1, parts):
        mine_row = jnp.where(me == d, group_rows[:, d * rows : (d + 1) * rows], mine_row)
    group_row = jnp.where(alive, mine_row, -1).astype(f32)
    group = jnp.broadcast_to(group_row, (8, rows)).T[:, :1]
    kind = lax.broadcasted_iota(jnp.int32, (rows, kinds), 1).astype(f32)
    onehot = (group == kind).astype(f32)
    ctf_rows = jnp.dot(onehot, ctf[...], precision=HIGH, preferred_element_type=f32)
    prec = precision[...]
    scale = prec * ctf_rows
    ctf_power = prec * jnp.square(ctf_rows)

    def window(source, c):
        begin = c * WIDE // 128 * 128
        end = min(-(-(c + 1) * WIDE // 128) * 128, source.shape[1])
        return source[:, begin:end], c * WIDE - begin

    bunches = [order[i * BUNCH : (i + 1) * BUNCH] for i in range(CYCLES // BUNCH)]
    for i, names in enumerate(bunches):
        lane_out = slice(i * BUNCH * BLOCK, (i + 1) * BUNCH * BLOCK)
        factor = jnp.concatenate(
            [jnp.broadcast_to(scale[:, c : c + 1], (rows, BLOCK)) for c in names], axis=1
        )
        pixels = [window(img, c) for c in names]
        for s in range(COARSE):
            piece = jnp.concatenate(
                [p[:, o + s * BLOCK : o + (s + 1) * BLOCK] for p, o in pixels], axis=1
            )
            value = (piece.astype(f32) * factor).astype(bf16)
            twice[s * rows : (s + 1) * rows, lane_out] = value
            if s < COARSE - 1:
                twice[(s + COARSE) * rows : (s + COARSE + 1) * rows, lane_out] = value

    fill = jnp.zeros((SLOT - classes, BUNCH * BLOCK), bf16)

    def turn_refs(s):
        for i, names in enumerate(bunches):
            lane_out = slice(i * BUNCH * BLOCK, (i + 1) * BUNCH * BLOCK)
            block = [window(refs, c) for c in names]
            for turn in range(FINE):
                pieces = []
                first = s * BLOCK - turn * TURN
                for b, o in block:
                    if first < 0:
                        pieces.append(b[:, o + WIDE + first : o + WIDE])
                        pieces.append(b[:, o : o + first + BLOCK])
                    else:
                        pieces.append(b[:, o + first : o + first + BLOCK])
                value = jnp.concatenate([jnp.concatenate(pieces, axis=1), fill], axis=0)
                turned[s, turn * SLOT : (turn + 1) * SLOT, lane_out] = value

    turn_refs(0)
    for s in range(COARSE):
        if s + 1 < COARSE:
            turn_refs(s + 1)
        product = lax.dot_general(
            twice[s * rows : (s + COARSE) * rows, :],
            turned[s],
            (((1,), (1,)), ((), ())),
            preferred_element_type=f32,
        )
        if s == 0:
            spread[...] = product
        else:
            spread[...] += product

    squares = jnp.zeros((SLOT, DEPTH), f32)
    for s in range(COARSE):
        wide = turned[s, :SLOT, :].astype(f32)
        squares = squares + wide * wide
    energies = [None] * CYCLES
    for i, c in enumerate(order):
        energies[c] = jnp.sum(squares[:, i * BLOCK : (i + 1) * BLOCK], axis=1, keepdims=True)
    energy = jnp.concatenate(energies, axis=1)
    ref_power = lax.dot_general(
        ctf_power, energy, (((1,), (1,)), ((), ())), precision=HIGH, preferred_element_type=f32
    )
    half = 0.5 * jnp.concatenate([ref_power] * FINE, axis=1)

    real = lax.broadcasted_iota(jnp.int32, (rows, FINE * SLOT), 1) % SLOT < classes
    highest = jnp.full((rows, FINE * SLOT), -jnp.inf, f32)
    for g in range(COARSE):
        part = slice(g * rows, (g + 1) * rows)
        logits = jnp.where(real, spread[part, :] - half, -jnp.inf)
        spread[part, :] = logits
        highest = jnp.maximum(highest, logits)
    peak = jnp.max(highest, axis=1, keepdims=True)
    total = jnp.zeros((rows, FINE * SLOT), f32)
    for g in range(COARSE):
        part = slice(g * rows, (g + 1) * rows)
        raised = jnp.exp(spread[part, :] - peak)
        spread[part, :] = raised
        total = total + raised
    mass = jnp.sum(total, axis=1, keepdims=True)
    lane = lax.broadcasted_iota(jnp.int32, (rows, 128), 1)
    stat_send[...] = jnp.where(lane == 0, peak, mass).T[:8, :]

    pl.semaphore_wait(barrier, quads - 1 + lines)
    stat_copies = []
    for step in range(1, quads):
        other = lax.rem(my_class + step, quads)
        copy = pltpu.make_async_remote_copy(
            src_ref=stat_send,
            dst_ref=stat_land.at[step - 1],
            send_sem=stat_ssem.at[step - 1],
            recv_sem=stat_rsem.at[step - 1],
            device_id=(me, other),
            device_id_type=MESH,
        )
        copy.start()
        stat_copies.append(copy)
    for copy in stat_copies:
        copy.wait()
    own_stat = stat_send[...]
    everyone = [own_stat] + [stat_land[i] for i in range(quads - 1)]
    top = everyone[0][:1]
    for stat in everyone[1:]:
        top = jnp.maximum(top, stat[:1])
    mass_total = jnp.zeros_like(top)
    for stat in everyone:
        mass_total = mass_total + stat[1:2] * jnp.exp(stat[:1] - top)
    conf[...] = jnp.where(alive, 1.0 / mass_total, 0.0)
    lower_by = jnp.where(alive, jnp.exp(own_stat[:1] - top) / mass_total, 0.0)
    times = jnp.broadcast_to(lower_by, (8, rows)).T[:, :1]

    total = jnp.zeros((rows, FINE * SLOT), f32)
    for g in range(COARSE):
        part = slice(g * rows, (g + 1) * rows)
        posterior = spread[part, :] * times
        spread[part, :] = posterior
        total = total + posterior
    chosen[...] = spread[...].T.astype(bf16)
    weight = total[:, :SLOT]
    for turn in range(1, FINE):
        weight = weight + total[:, turn * SLOT : (turn + 1) * SLOT]
    den = jnp.dot(weight.T, ctf_power, precision=HIGH, preferred_element_type=f32)
    den_mine[...] = jnp.concatenate([den, jnp.zeros((SLOT, 128 - CYCLES), f32)], axis=1)
    den_copy = pltpu.make_async_remote_copy(
        src_ref=den_mine,
        dst_ref=den_take,
        send_sem=den_ssem.at[0],
        recv_sem=den_rsem.at[0],
        device_id=(mate, my_class),
        device_id_type=MESH,
    )
    den_copy.start()

    def give_copy(s):
        return pltpu.make_async_remote_copy(
            src_ref=give.at[s],
            dst_ref=take.at[s],
            send_sem=give_ssem.at[s],
            recv_sem=give_rsem.at[s],
            device_id=(mate, my_class),
            device_id_type=MESH,
        )

    def emit(s, value):
        left, right = value[:classes, :half_depth], value[:classes, half_depth:]
        mine[s] = jnp.where(low == 0, left, right)
        give[s] = jnp.where(low == 0, right, left).astype(bf16)
        give_copy(s).start()

    def pass_copy(j, step):
        other = 2 * lax.rem(high + step, lines) + low
        return pltpu.make_async_remote_copy(
            src_ref=pass_on.at[j, step],
            dst_ref=land.at[j, step - 1],
            send_sem=pass_ssem.at[j, step - 1],
            recv_sem=pass_rsem.at[j, step - 1],
            device_id=(other, my_class),
            device_id_type=MESH,
        )

    wide_pair = pass_on.shape[-1]
    groups = [[s for s in (2 * j, 2 * j + 1) if s < COARSE] for j in range((COARSE + 1) // 2)]

    def forward(j):
        sums = []
        for s in groups[j]:
            give_copy(s).wait_recv()
            sums.append(mine[s] + take[s].astype(f32))
        last = j == len(groups) - 1
        if last:
            den_copy.wait_recv()
            den_all = den_mine[...] + den_take[...]
        for h in range(lines):
            pieces = [v[:, h * share * BLOCK : (h + 1) * share * BLOCK].astype(bf16) for v in sums]
            if last:
                near = den_all[:classes, 2 * h * share : (2 * h + 1) * share]
                far = den_all[:classes, (2 * h + 1) * share : (2 * h + 2) * share]
                some = jnp.where(low == 0, near, far)
                upper = some.astype(bf16)
                pieces += [upper, (some - upper.astype(f32)).astype(bf16)]
            used = sum(p.shape[1] for p in pieces)
            if used < wide_pair:
                pieces.append(jnp.zeros((classes, wide_pair - used), bf16))
            pass_on[j, lax.rem(h - high + lines, lines)] = jnp.concatenate(pieces, axis=1)
        for step in range(1, lines):
            pass_copy(j, step).start()

    chunk = BUNCH * BLOCK
    place = lax.broadcasted_iota(jnp.int32, (SLOT, chunk), 1) % BLOCK
    for s in range(COARSE + 1):

        @pl.loop(0, DEPTH // chunk)
        def _(n):
            columns = pl.ds(pl.multiple_of(n * chunk, 128), chunk)
            if s > 0:
                old = fresh.at[(s - 1) % 2]
                stay = old[:SLOT, columns]
                beyond = jnp.zeros((SLOT, chunk), f32)
                for turn in range(1, FINE):
                    moved = pltpu.roll(
                        old[turn * SLOT : (turn + 1) * SLOT, columns], chunk - turn * TURN, 1
                    )
                    inside = place < BLOCK - turn * TURN
                    stay = stay + jnp.where(inside, moved, 0.0)
                    beyond = beyond + jnp.where(inside, 0.0, moved)
                beyond = pltpu.roll(beyond, BLOCK, 1)
                if s == 1:
                    first_over[:, columns] = beyond
                else:
                    over[:, columns] = kept[:, columns] + beyond
                kept[:, columns] = stay
            if s < COARSE:
                fresh[s % 2, :, columns] = jnp.dot(
                    chosen[...],
                    twice[s * rows : (s + COARSE) * rows, columns],
                    preferred_element_type=f32,
                )

        if s > 1:
            emit(s - 2, over[...])
        if s == COARSE:
            emit(COARSE - 1, kept[...] + first_over[...])
        if s >= 5 and s % 2 == 1 and s // 2 - 2 < len(groups) - 2:
            forward(s // 2 - 2)
    for j in range(len(groups) - 2, len(groups)):
        forward(j)

    totals = []
    for j in range(len(groups)):
        value = pass_on[j, 0].astype(f32)
        for step in range(1, lines):
            pass_copy(j, step).wait_recv()
            value = value + land[j, step - 1].astype(f32)
        totals.append(value)
    end = share * BLOCK
    tail = totals[-1]
    den_sum = tail[:, end : end + share] + tail[:, end + share : end + 2 * share]
    cycles = []
    for c in range(share):
        numerator = jnp.concatenate(
            [
                totals[s // 2][
                    :, ((s % 2) * share + c) * BLOCK : ((s % 2) * share + c + 1) * BLOCK
                ]
                for s in range(COARSE)
            ],
            axis=1,
        )
        cycles.append(numerator / (den_sum[:, c : c + 1] + ridge_term))
    out[...] = jnp.concatenate(cycles, axis=1)

    den_copy.wait_send()
    for s in range(COARSE):
        give_copy(s).wait_send()
    for j in range(len(groups)):
        for step in range(1, lines):
            pass_copy(j, step).wait_send()


def body(images, pick_counts, group_of, ctf_table, precision, references):
    parts = lax.axis_size("dom")
    quads = lax.axis_size("cls")
    rows = images.shape[0]
    classes = references.shape[0]
    share = CYCLES // parts
    lines = parts // 2
    pairs = (COARSE + 1) // 2
    wide_pair = -(-max(2 * share * BLOCK, share * (BLOCK + 2)) // 128) * 128
    dma = pltpu.SemaphoreType.DMA
    new_refs, confidence = pl.pallas_call(
        functools.partial(em_kernel, parts, quads),
        out_shape=[
            jax.ShapeDtypeStruct((classes, share * WIDE), f32),
            jax.ShapeDtypeStruct((1, rows), f32),
        ],
        in_specs=[pl.BlockSpec(memory_space=pltpu.VMEM)] * 6,
        out_specs=[pl.BlockSpec(memory_space=pltpu.VMEM)] * 2,
        scratch_shapes=[
            pltpu.VMEM(((2 * COARSE - 1) * rows, DEPTH), bf16),
            pltpu.VMEM((COARSE, FINE * SLOT, DEPTH), bf16),
            pltpu.VMEM((COARSE * rows, FINE * SLOT), f32),
            pltpu.VMEM((FINE * SLOT, COARSE * rows), bf16),
            pltpu.VMEM((2, FINE * SLOT, DEPTH), f32),
            pltpu.VMEM((SLOT, DEPTH), f32),
            pltpu.VMEM((SLOT, DEPTH), f32),
            pltpu.VMEM((SLOT, DEPTH), f32),
            pltpu.VMEM((COARSE, classes, DEPTH // 2), f32),
            pltpu.VMEM((COARSE, classes, DEPTH // 2), bf16),
            pltpu.VMEM((COARSE, classes, DEPTH // 2), bf16),
            pltpu.VMEM((SLOT, 128), f32),
            pltpu.VMEM((SLOT, 128), f32),
            pltpu.VMEM((pairs, lines, classes, wide_pair), bf16),
            pltpu.VMEM((pairs, lines - 1, classes, wide_pair), bf16),
            pltpu.VMEM((8, rows), f32),
            pltpu.VMEM((quads - 1, 8, rows), f32),
            dma((quads - 1,)),
            dma((quads - 1,)),
            dma((COARSE,)),
            dma((COARSE,)),
            dma((1,)),
            dma((1,)),
            dma((pairs, lines - 1)),
            dma((pairs, lines - 1)),
        ],
        compiler_params=pltpu.CompilerParams(
            vmem_limit_bytes=56 * 2**20, collective_id=0, has_side_effects=True
        ),
        name="em",
    )(
        images,
        pick_counts[None, :],
        group_of[None, :],
        ctf_table,
        precision[None, :],
        references,
    )
    return (new_refs, confidence.reshape(rows))


def solution(mesh):
    return jax.shard_map(
        body,
        mesh=mesh,
        in_specs=(P("dom", None), P(), P(), P(), P(), P("cls", None)),
        out_specs=(P("cls", "dom"), P("dom")),
        check_vma=False,
    )
```

```python
import functools

import jax
import jax.numpy as jnp
from jax import lax
from jax.experimental import pallas as pl
from jax.experimental.pallas import tpu as pltpu
from jax.sharding import PartitionSpec as P

CYCLES = 32
WIDE = 432
TURN = 12
FINE = 4
BLOCK = TURN * FINE
COARSE = WIDE // BLOCK
BUNCH = 8
DEPTH = CYCLES * BLOCK
SLOT = 64
ridge_term = 0.02
HIGH = lax.Precision.HIGHEST
f32 = jnp.float32
bf16 = jnp.bfloat16

MESH = pl.DeviceIdType.MESH


def em_kernel(
    parts,
    quads,
    img,
    counts,
    group_rows,
    ctf,
    precision,
    refs,
    out,
    conf,
    twice,
    turned,
    spread,
    chosen,
    fresh,
    kept,
    over,
    first_over,
    mine,
    give,
    take,
    den_mine,
    den_take,
    pass_on,
    land,
    stat_send,
    stat_land,
    stat_ssem,
    stat_rsem,
    give_ssem,
    give_rsem,
    den_ssem,
    den_rsem,
    pass_ssem,
    pass_rsem,
):
    rows = img.shape[0]
    classes = refs.shape[0]
    kinds = ctf.shape[0]
    share = CYCLES // parts
    lines = parts // 2
    half_depth = DEPTH // 2
    me = lax.axis_index("dom")
    my_class = lax.axis_index("cls")
    low, high = lax.rem(me, 2), lax.div(me, 2)
    mate = me + 1 - 2 * low

    barrier = pltpu.get_barrier_semaphore()
    for step in range(1, quads):
        other = lax.rem(my_class + step, quads)
        pl.semaphore_signal(barrier, inc=1, device_id=(me, other), device_id_type=MESH)
    pl.semaphore_signal(barrier, inc=1, device_id=(mate, my_class), device_id_type=MESH)
    for step in range(1, lines):
        other = 2 * lax.rem(high + step, lines) + low
        pl.semaphore_signal(barrier, inc=1, device_id=(other, my_class), device_id_type=MESH)

    order = [
        (h * 2 + l) * share + c for l in range(2) for h in range(lines) for c in range(share)
    ]

    count_lane = lax.broadcasted_iota(jnp.int32, (1, parts), 1)
    count = jnp.sum(jnp.where(count_lane == me, counts[...], 0), axis=1, keepdims=True)
    alive = lax.broadcasted_iota(jnp.int32, (1, rows), 1) < count
    mine_row = group_rows[:, :rows]
    for d in range(1, parts):
        mine_row = jnp.where(me == d, group_rows[:, d * rows : (d + 1) * rows], mine_row)
    group_row = jnp.where(alive, mine_row, -1).astype(f32)
    group = jnp.broadcast_to(group_row, (8, rows)).T[:, :1]
    kind = lax.broadcasted_iota(jnp.int32, (rows, kinds), 1).astype(f32)
    onehot = (group == kind).astype(f32)
    ctf_rows = jnp.dot(onehot, ctf[...], precision=HIGH, preferred_element_type=f32)
    prec = precision[...]
    scale = prec * ctf_rows
    ctf_power = prec * jnp.square(ctf_rows)

    def window(source, c):
        begin = c * WIDE // 128 * 128
        end = min(-(-(c + 1) * WIDE // 128) * 128, source.shape[1])
        return source[:, begin:end], c * WIDE - begin

    bunches = [order[i * BUNCH : (i + 1) * BUNCH] for i in range(CYCLES // BUNCH)]
    for i, names in enumerate(bunches):
        lane_out = slice(i * BUNCH * BLOCK, (i + 1) * BUNCH * BLOCK)
        factor = jnp.concatenate(
            [jnp.broadcast_to(scale[:, c : c + 1], (rows, BLOCK)) for c in names], axis=1
        )
        pixels = [window(img, c) for c in names]
        for s in range(COARSE):
            piece = jnp.concatenate(
                [p[:, o + s * BLOCK : o + (s + 1) * BLOCK] for p, o in pixels], axis=1
            )
            value = (piece.astype(f32) * factor).astype(bf16)
            twice[s * rows : (s + 1) * rows, lane_out] = value
            if s < COARSE - 1:
                twice[(s + COARSE) * rows : (s + COARSE + 1) * rows, lane_out] = value

    fill = jnp.zeros((SLOT - classes, BUNCH * BLOCK), bf16)

    def turn_refs(s):
        for i, names in enumerate(bunches):
            lane_out = slice(i * BUNCH * BLOCK, (i + 1) * BUNCH * BLOCK)
            block = [window(refs, c) for c in names]
            for turn in range(FINE):
                pieces = []
                first = s * BLOCK - turn * TURN
                for b, o in block:
                    if first < 0:
                        pieces.append(b[:, o + WIDE + first : o + WIDE])
                        pieces.append(b[:, o : o + first + BLOCK])
                    else:
                        pieces.append(b[:, o + first : o + first + BLOCK])
                value = jnp.concatenate([jnp.concatenate(pieces, axis=1), fill], axis=0)
                turned[s, turn * SLOT : (turn + 1) * SLOT, lane_out] = value

    turn_refs(0)
    for s in range(COARSE):
        if s + 1 < COARSE:
            turn_refs(s + 1)
        product = lax.dot_general(
            twice[s * rows : (s + COARSE) * rows, :],
            turned[s],
            (((1,), (1,)), ((), ())),
            preferred_element_type=f32,
        )
        if s == 0:
            spread[...] = product
        else:
            spread[...] += product

    squares = jnp.zeros((SLOT, DEPTH), f32)
    for s in range(COARSE):
        wide = turned[s, :SLOT, :].astype(f32)
        squares = squares + wide * wide
    energies = [None] * CYCLES
    for i, c in enumerate(order):
        energies[c] = jnp.sum(squares[:, i * BLOCK : (i + 1) * BLOCK], axis=1, keepdims=True)
    energy = jnp.concatenate(energies, axis=1)
    ref_power = lax.dot_general(
        ctf_power, energy, (((1,), (1,)), ((), ())), precision=HIGH, preferred_element_type=f32
    )
    half = 0.5 * jnp.concatenate([ref_power] * FINE, axis=1)

    real = lax.broadcasted_iota(jnp.int32, (rows, FINE * SLOT), 1) % SLOT < classes
    highest = jnp.full((rows, FINE * SLOT), -jnp.inf, f32)
    for g in range(COARSE):
        part = slice(g * rows, (g + 1) * rows)
        logits = jnp.where(real, spread[part, :] - half, -jnp.inf)
        spread[part, :] = logits
        highest = jnp.maximum(highest, logits)
    peak = jnp.max(highest, axis=1, keepdims=True)
    total = jnp.zeros((rows, FINE * SLOT), f32)
    for g in range(COARSE):
        part = slice(g * rows, (g + 1) * rows)
        raised = jnp.exp(spread[part, :] - peak)
        spread[part, :] = raised
        total = total + raised
    mass = jnp.sum(total, axis=1, keepdims=True)
    lane = lax.broadcasted_iota(jnp.int32, (rows, 128), 1)
    stat_send[...] = jnp.where(lane == 0, peak, mass).T[:8, :]

    pl.semaphore_wait(barrier, quads - 1 + lines)
    stat_copies = []
    for step in range(1, quads):
        other = lax.rem(my_class + step, quads)
        copy = pltpu.make_async_remote_copy(
            src_ref=stat_send,
            dst_ref=stat_land.at[step - 1],
            send_sem=stat_ssem.at[step - 1],
            recv_sem=stat_rsem.at[step - 1],
            device_id=(me, other),
            device_id_type=MESH,
        )
        copy.start()
        stat_copies.append(copy)
    for copy in stat_copies:
        copy.wait()
    own_stat = stat_send[...]
    everyone = [own_stat] + [stat_land[i] for i in range(quads - 1)]
    top = everyone[0][:1]
    for stat in everyone[1:]:
        top = jnp.maximum(top, stat[:1])
    mass_total = jnp.zeros_like(top)
    for stat in everyone:
        mass_total = mass_total + stat[1:2] * jnp.exp(stat[:1] - top)
    conf[...] = jnp.where(alive, 1.0 / mass_total, 0.0)
    lower_by = jnp.where(alive, jnp.exp(own_stat[:1] - top) / mass_total, 0.0)
    times = jnp.broadcast_to(lower_by, (8, rows)).T[:, :1]

    total = jnp.zeros((rows, FINE * SLOT), f32)
    for g in range(COARSE):
        part = slice(g * rows, (g + 1) * rows)
        posterior = spread[part, :] * times
        spread[part, :] = posterior
        total = total + posterior
    chosen[...] = spread[...].T.astype(bf16)
    weight = total[:, :SLOT]
    for turn in range(1, FINE):
        weight = weight + total[:, turn * SLOT : (turn + 1) * SLOT]
    den = jnp.dot(weight.T, ctf_power, precision=HIGH, preferred_element_type=f32)
    den_mine[...] = jnp.concatenate([den, jnp.zeros((SLOT, 128 - CYCLES), f32)], axis=1)
    den_copy = pltpu.make_async_remote_copy(
        src_ref=den_mine,
        dst_ref=den_take,
        send_sem=den_ssem.at[0],
        recv_sem=den_rsem.at[0],
        device_id=(mate, my_class),
        device_id_type=MESH,
    )
    den_copy.start()

    def give_copy(s):
        return pltpu.make_async_remote_copy(
            src_ref=give.at[s],
            dst_ref=take.at[s],
            send_sem=give_ssem.at[s],
            recv_sem=give_rsem.at[s],
            device_id=(mate, my_class),
            device_id_type=MESH,
        )

    def emit(s, value):
        left, right = value[:classes, :half_depth], value[:classes, half_depth:]
        mine[s] = jnp.where(low == 0, left, right)
        give[s] = jnp.where(low == 0, right, left).astype(bf16)
        give_copy(s).start()

    def pass_copy(j, step):
        other = 2 * lax.rem(high + step, lines) + low
        return pltpu.make_async_remote_copy(
            src_ref=pass_on.at[j, step],
            dst_ref=land.at[j, step - 1],
            send_sem=pass_ssem.at[j, step - 1],
            recv_sem=pass_rsem.at[j, step - 1],
            device_id=(other, my_class),
            device_id_type=MESH,
        )

    wide_pair = pass_on.shape[-1]
    groups = [[s for s in (2 * j, 2 * j + 1) if s < COARSE] for j in range((COARSE + 1) // 2)]

    def forward(j):
        sums = []
        for s in groups[j]:
            give_copy(s).wait_recv()
            sums.append(mine[s] + take[s].astype(f32))
        last = j == len(groups) - 1
        if last:
            den_copy.wait_recv()
            den_all = den_mine[...] + den_take[...]
        for h in range(lines):
            pieces = [v[:, h * share * BLOCK : (h + 1) * share * BLOCK].astype(bf16) for v in sums]
            if last:
                near = den_all[:classes, 2 * h * share : (2 * h + 1) * share]
                far = den_all[:classes, (2 * h + 1) * share : (2 * h + 2) * share]
                some = jnp.where(low == 0, near, far)
                upper = some.astype(bf16)
                pieces += [upper, (some - upper.astype(f32)).astype(bf16)]
            used = sum(p.shape[1] for p in pieces)
            if used < wide_pair:
                pieces.append(jnp.zeros((classes, wide_pair - used), bf16))
            pass_on[j, lax.rem(h - high + lines, lines)] = jnp.concatenate(pieces, axis=1)
        for step in range(1, lines):
            pass_copy(j, step).start()

    chunk = BUNCH * BLOCK
    place = lax.broadcasted_iota(jnp.int32, (SLOT, chunk), 1) % BLOCK
    for s in range(COARSE + 1):
        for n in range(DEPTH // chunk):
            columns = slice(n * chunk, (n + 1) * chunk)
            if s > 0:
                old = (s - 1) % 2
                stay = fresh[old, :SLOT, columns]
                beyond = jnp.zeros((SLOT, chunk), f32)
                for turn in range(1, FINE):
                    moved = pltpu.roll(
                        fresh[old, turn * SLOT : (turn + 1) * SLOT, columns],
                        chunk - turn * TURN,
                        1,
                    )
                    inside = place < BLOCK - turn * TURN
                    stay = stay + jnp.where(inside, moved, 0.0)
                    beyond = beyond + jnp.where(inside, 0.0, moved)
                beyond = pltpu.roll(beyond, BLOCK, 1)
                if s == 1:
                    first_over[:, columns] = beyond
                else:
                    over[:, columns] = kept[:, columns] + beyond
                kept[:, columns] = stay
            if s < COARSE:
                fresh[s % 2, :, columns] = jnp.dot(
                    chosen[...],
                    twice[s * rows : (s + COARSE) * rows, columns],
                    preferred_element_type=f32,
                )

        if s > 1:
            emit(s - 2, over[...])
        if s == COARSE:
            emit(COARSE - 1, kept[...] + first_over[...])
        if s >= 5 and s % 2 == 1 and s // 2 - 2 < len(groups) - 2:
            forward(s // 2 - 2)
    for j in range(len(groups) - 2, len(groups)):
        forward(j)

    totals = []
    for j in range(len(groups)):
        value = pass_on[j, 0].astype(f32)
        for step in range(1, lines):
            pass_copy(j, step).wait_recv()
            value = value + land[j, step - 1].astype(f32)
        totals.append(value)
    end = share * BLOCK
    tail = totals[-1]
    den_sum = tail[:, end : end + share] + tail[:, end + share : end + 2 * share]
    cycles = []
    for c in range(share):
        numerator = jnp.concatenate(
            [
                totals[s // 2][
                    :, ((s % 2) * share + c) * BLOCK : ((s % 2) * share + c + 1) * BLOCK
                ]
                for s in range(COARSE)
            ],
            axis=1,
        )
        cycles.append(numerator / (den_sum[:, c : c + 1] + ridge_term))
    out[...] = jnp.concatenate(cycles, axis=1)

    den_copy.wait_send()
    for s in range(COARSE):
        give_copy(s).wait_send()
    for j in range(len(groups)):
        for step in range(1, lines):
            pass_copy(j, step).wait_send()


def body(images, pick_counts, group_of, ctf_table, precision, references):
    parts = lax.axis_size("dom")
    quads = lax.axis_size("cls")
    rows = images.shape[0]
    classes = references.shape[0]
    share = CYCLES // parts
    lines = parts // 2
    pairs = (COARSE + 1) // 2
    wide_pair = -(-max(2 * share * BLOCK, share * (BLOCK + 2)) // 128) * 128
    dma = pltpu.SemaphoreType.DMA
    new_refs, confidence = pl.pallas_call(
        functools.partial(em_kernel, parts, quads),
        out_shape=[
            jax.ShapeDtypeStruct((classes, share * WIDE), f32),
            jax.ShapeDtypeStruct((1, rows), f32),
        ],
        in_specs=[pl.BlockSpec(memory_space=pltpu.VMEM)] * 6,
        out_specs=[pl.BlockSpec(memory_space=pltpu.VMEM)] * 2,
        scratch_shapes=[
            pltpu.VMEM(((2 * COARSE - 1) * rows, DEPTH), bf16),
            pltpu.VMEM((COARSE, FINE * SLOT, DEPTH), bf16),
            pltpu.VMEM((COARSE * rows, FINE * SLOT), f32),
            pltpu.VMEM((FINE * SLOT, COARSE * rows), bf16),
            pltpu.VMEM((2, FINE * SLOT, DEPTH), f32),
            pltpu.VMEM((SLOT, DEPTH), f32),
            pltpu.VMEM((SLOT, DEPTH), f32),
            pltpu.VMEM((SLOT, DEPTH), f32),
            pltpu.VMEM((COARSE, classes, DEPTH // 2), f32),
            pltpu.VMEM((COARSE, classes, DEPTH // 2), bf16),
            pltpu.VMEM((COARSE, classes, DEPTH // 2), bf16),
            pltpu.VMEM((SLOT, 128), f32),
            pltpu.VMEM((SLOT, 128), f32),
            pltpu.VMEM((pairs, lines, classes, wide_pair), bf16),
            pltpu.VMEM((pairs, lines - 1, classes, wide_pair), bf16),
            pltpu.VMEM((8, rows), f32),
            pltpu.VMEM((quads - 1, 8, rows), f32),
            dma((quads - 1,)),
            dma((quads - 1,)),
            dma((COARSE,)),
            dma((COARSE,)),
            dma((1,)),
            dma((1,)),
            dma((pairs, lines - 1)),
            dma((pairs, lines - 1)),
        ],
        compiler_params=pltpu.CompilerParams(
            vmem_limit_bytes=56 * 2**20, collective_id=0, has_side_effects=True
        ),
        name="em",
    )(
        images,
        pick_counts[None, :],
        group_of[None, :],
        ctf_table,
        precision[None, :],
        references,
    )
    return (new_refs, confidence.reshape(rows))


def solution(mesh):
    return jax.shard_map(
        body,
        mesh=mesh,
        in_specs=(P("dom", None), P(), P(), P(), P(), P("cls", None)),
        out_specs=(P("cls", "dom"), P("dom")),
        check_vma=False,
    )
```
